32 devices in a mesh: heads: 2 (over y), groups: 16 (over z, x, core).
Axes of the slice: x: 2, y: 2, z: 4, core: 2. Of those that a mesh axis runs over, the one named last changes fastest.
Arguments:
- hidden_rows: bfloat16 [192, 8192], P(None, 'groups'), may hold values from -6 to 6
- qkv_weight: bfloat16 [8192, 10240], P('groups', 'heads'), may hold values from -1 to 1
- out_weight: bfloat16 [8192, 8192], P('heads', 'groups'), may hold values from -0.0625 to 0.0625
- norm_gain: float32 [8192], P('groups'), may hold values from 0.5 to 1.5
- next_weight: bfloat16 [8192, 10240], P('groups', 'heads'), may hold values from -0.0625 to 0.0625
- cache_keys: bfloat16 [12288, 1024], P('groups', 'heads'), may hold values from -6 to 6
- cache_values: bfloat16 [12288, 1024], P('groups', 'heads'), may hold values from -6 to 6
- group_lengths: int32 [32], replicated, may hold values from 128 to 384, as said below
- group_owner: int32 [32], replicated, may hold values from 0 to 15, as said below
- group_start: int32 [32], replicated, may hold values from 0 to 8064, as said below
- listed_rows: int32 [192], replicated, may hold values from 0 to 8191, as said below
Outputs:
- hidden_out: bfloat16 [192, 8192], P(None, 'groups')
- next_qkv: bfloat16 [192, 10240], P('groups', 'heads')
The draws below stay inside these ranges and needn't reach their ends.
Inputs may be any that keep to these rules, and one draw needn't show every extreme that they name: `group_lengths`: multiples of 128; groups 2k and 2k+1 together hold 512 tokens. `group_owner`: group 2k is held by owner k; every owner holds exactly two groups; one owner holds 768 tokens. The intervals from group_start to group_start + group_lengths - 1 of all groups tile 0 to 8191. `listed_rows`: distinct and increasing.
All inputs are finite; a program needn't handle non-finite values.
Results may differ from the reference program's by a relative error of at most 0.0085.
Values may be sent and summed in bfloat16 or wider, within the bound.
A program may use at most 128 MiB of HBM per device.

```python
import jax
import jax.numpy as jnp
from jax import lax

D = 8192
KVH = 8
HD = 128
GQ = 8
BLK = 128
PAIR = 4
R = 192
CAP = 768
SEQ = 8192
N_GROUPS = 16


def draw_hidden_rows(key, part):
    rows = jnp.clip(jax.random.normal(jax.random.fold_in(key, 301), (R, D), jnp.float32), -6.0, 6.0)
    return jnp.clip(rows, -6.0, 6.0).astype(jnp.bfloat16)


def draw_qkv_weight(key, part):
    weights = jnp.clip(jax.random.normal(jax.random.fold_in(key, 302), (D, KVH * (GQ + 2) * HD), jnp.float32), -6.0, 6.0) * D ** (-0.5)
    return jnp.clip(weights, -1.0, 1.0).astype(jnp.bfloat16)


def draw_cache_keys(key, part):
    total_rows = N_GROUPS * CAP
    rows = jnp.clip(jax.random.normal(jax.random.fold_in(key, 303), (total_rows, KVH * HD), jnp.float32), -6.0, 6.0)
    return rows.astype(jnp.bfloat16)


def group_layout(key):
    base = jax.random.fold_in(key, 91)
    streams = jax.random.split(base, 5)
    count = N_GROUPS
    leading = jax.random.randint(streams[0], (count,), 1, PAIR)
    widest = jax.random.randint(streams[1], (), 0, count)
    partner = (widest + 1 + jax.random.randint(streams[2], (), 0, count - 1)) % count
    leading = leading.at[widest].set(PAIR - 1).at[partner].set(1)
    mapping = jax.random.permutation(streams[3], count)
    where_widest = jnp.argmax(mapping == widest)
    moved = mapping[partner]
    mapping = mapping.at[where_widest].set(moved).at[partner].set(widest)
    lengths = jnp.stack([leading, PAIR - leading], axis=1).reshape(2 * count) * BLK
    owners = jnp.stack([jnp.arange(count), mapping], axis=1).reshape(2 * count)
    order = jax.random.permutation(streams[4], 2 * count)
    ordered = lengths[order]
    sorted_starts = jnp.cumsum(ordered) - ordered
    starts = jnp.zeros((2 * count,), jnp.int32).at[order].set(sorted_starts.astype(jnp.int32))
    return (lengths.astype(jnp.int32), owners.astype(jnp.int32), starts.astype(jnp.int32))


def draw_group_lengths(key, part):
    return group_layout(key)[0]


def draw_group_owner(key, part):
    return group_layout(key)[1]


def draw_group_start(key, part):
    return group_layout(key)[2]


def draw_listed_rows(key, part):
    shuffled = jax.random.permutation(jax.random.fold_in(key, 17), SEQ)
    return jnp.sort(shuffled[:R]).astype(jnp.int32)


def block_levels(rng, shape, shards, smallest, largest):
    loudness = 1.0
    for position, shards_of in shards:
        steps = jax.random.uniform(jax.random.fold_in(jax.random.fold_in(rng, 6), position), (shards_of,), jnp.float32, smallest / len(shards), largest / len(shards))
        loudness = loudness * jnp.repeat(jnp.exp(steps), shape[position] // shards_of).reshape((-1,) + (1,) * (len(shape) - 1 - position))
    return loudness


def centred(stream_key, dims, deviation, most, shards=(), held_as=jnp.bfloat16):
    drawn = deviation * jax.random.normal(stream_key, dims, jnp.float32)
    if shards:
        drawn = drawn * block_levels(stream_key, dims, shards, -0.22, 0.18)
    return jnp.clip(drawn, -most, most).astype(held_as)


def setup_inputs(seed: int = 0) -> dict:
    key_of = jax.random.split(jax.random.key(seed), 12)
    hidden_rows = draw_hidden_rows(jax.random.fold_in(key_of[11], 71), 0)
    qkv_weight = draw_qkv_weight(jax.random.fold_in(key_of[11], 71), 0)
    out_weight = centred(key_of[2], (KVH * GQ * HD, D), (KVH * GQ * HD) ** -0.5, 0.0625, ((0, 2), (1, 16)))
    norm_gain = jnp.clip(1.0 + 0.1 * jax.random.normal(key_of[3], (D,), jnp.float32), 0.5, 1.5)
    next_weight = centred(key_of[4], (D, KVH * (GQ + 2) * HD), D ** -0.5, 0.0625, ((0, 16), (1, 2)))
    cache_keys = draw_cache_keys(jax.random.fold_in(key_of[11], 71), 0)
    cache_values = centred(key_of[6], (N_GROUPS * CAP, KVH * HD), 1.0, 6.0, ((0, 16), (1, 2)))
    group_lengths = draw_group_lengths(jax.random.fold_in(key_of[11], 71), 0)
    group_owner = draw_group_owner(jax.random.fold_in(key_of[11], 71), 0)
    group_start = draw_group_start(jax.random.fold_in(key_of[11], 71), 0)
    listed_rows = draw_listed_rows(jax.random.fold_in(key_of[11], 71), 0)
    return dict(hidden_rows=hidden_rows, qkv_weight=qkv_weight, out_weight=out_weight, norm_gain=norm_gain, next_weight=next_weight, cache_keys=cache_keys, cache_values=cache_values, group_lengths=group_lengths, group_owner=group_owner, group_start=group_start, listed_rows=listed_rows)


theta_base = 500000.0
epsilon = 1e-05
masked_score = -1e+30

def angles(positions, half_dim):
    freq = theta_base ** (-(jnp.arange(half_dim).astype(jnp.float32) * 2.0 / (2 * half_dim)))
    phase = positions.astype(jnp.float32)[:, None] * freq[None, :]
    return (jnp.cos(phase), jnp.sin(phase))

def rotate(vectors, cosine, sine):
    half_dim = vectors.shape[-1] // 2
    lower = vectors[..., :half_dim]
    upper = vectors[..., half_dim:]
    return jnp.concatenate([lower * cosine - upper * sine, upper * cosine + lower * sine], axis=-1)

def layout(owner_index, group_lengths, group_owner, group_start, listed_rows, cap_blocks, block_rows):
    block_len = (group_lengths // block_rows).astype(jnp.int32)
    holder = (group_owner == owner_index).astype(jnp.int32)
    held_blocks = holder * block_len
    offset = (jnp.cumsum(held_blocks) - held_blocks).astype(jnp.int32)
    block_ids = jnp.arange(cap_blocks).astype(jnp.int32)[:, None]
    member = ((holder[None, :] == 1) & (block_ids >= offset[None, :]) & (block_ids < offset[None, :] + block_len[None, :])).astype(jnp.int32)
    shift_blk = lax.optimization_barrier(jnp.sum(member * group_start[None, :], axis=1)).astype(jnp.int32)
    begin_blk = lax.optimization_barrier(jnp.sum(member * (group_start[None, :] + (block_ids - offset[None, :]) * block_rows), axis=1)).astype(jnp.int32)
    live_blk = lax.optimization_barrier(jnp.sum(member, axis=1)) > 0
    inside = jnp.arange(block_rows).astype(jnp.int32)[None, :]
    key_pos = (begin_blk[:, None] + inside).reshape(-1)
    key_shift = (shift_blk[:, None] + 0 * inside).reshape(-1)
    key_live = (live_blk[:, None] & (inside >= 0)).reshape(-1)
    listed_hit = jnp.any(key_pos[:, None] == listed_rows[None, :], axis=1)
    return (key_pos, key_shift, key_live & jnp.logical_not(listed_hit))

def combine(first_part, second_part):
    peak_one, total_one, numer_one = first_part
    peak_two, total_two, numer_two = second_part
    highest = jnp.maximum(peak_one, peak_two)
    scale_one = jnp.exp(peak_one - highest)
    scale_two = jnp.exp(peak_two - highest)
    return (highest, total_one * scale_one + total_two * scale_two, numer_one * scale_one[..., None] + numer_two * scale_two[..., None])

def owner_partial(owner_index, queries, keys_new, values_new, cache_keys, cache_values, group_lengths, group_owner, group_start, listed_rows):
    local_rows = R // N_GROUPS
    key_pos, key_shift, key_live = layout(owner_index, group_lengths, group_owner, group_start, listed_rows, CAP // BLK, BLK)
    slab_keys = lax.dynamic_slice_in_dim(cache_keys, owner_index * CAP, CAP).astype(jnp.float32).reshape(CAP, KVH, HD)
    cosine, sine = angles(key_shift, HD // 2)
    rotated = rotate(slab_keys, cosine[:, None], sine[:, None]).astype(jnp.bfloat16)
    slab_values = lax.dynamic_slice_in_dim(cache_values, owner_index * CAP, CAP).reshape(CAP, KVH, HD)
    first_row = owner_index * local_rows
    own_keys = lax.dynamic_slice_in_dim(keys_new, first_row, local_rows)
    own_values = lax.dynamic_slice_in_dim(values_new, first_row, local_rows)
    own_pos = lax.dynamic_slice_in_dim(listed_rows, first_row, local_rows).astype(jnp.int32)
    all_keys = jnp.concatenate([rotated, own_keys], axis=0).astype(jnp.float32)
    all_values = jnp.concatenate([slab_values, own_values], axis=0).astype(jnp.float32)
    all_pos = jnp.concatenate([key_pos.astype(jnp.int32), own_pos], axis=0)
    all_live = jnp.concatenate([key_live, jnp.ones((local_rows,), bool)], axis=0)
    scores = jnp.einsum('rhgd,khd->rhgk', queries.astype(jnp.float32), all_keys) * HD ** (-0.5)
    allowed = (all_live[None, :] & (all_pos[None, :] <= listed_rows[:, None]))[:, None, None, :]
    scores = jnp.where(allowed, scores, masked_score)
    peaks = lax.optimization_barrier(jnp.max(scores, axis=-1))
    weights = jnp.where(allowed, jnp.exp(scores - peaks[..., None]), 0.0)
    totals = lax.optimization_barrier(jnp.sum(weights, axis=-1))
    rounded = lax.optimization_barrier(weights.astype(jnp.bfloat16))
    numerator = jnp.einsum('rhgk,khd->rhgd', rounded.astype(jnp.float32), all_values)
    return (peaks, totals, numerator)

def reference(hidden_rows, qkv_weight, out_weight, norm_gain, next_weight, cache_keys, cache_values, group_lengths, group_owner, group_start, listed_rows):
    mixed = jnp.dot(hidden_rows, qkv_weight, preferred_element_type=jnp.float32).reshape(R, KVH, GQ + 2, HD)
    cosine, sine = angles(listed_rows, HD // 2)
    queries = rotate(mixed[:, :, :GQ], cosine[:, None, None], sine[:, None, None]).astype(jnp.bfloat16)
    keys_new = rotate(mixed[:, :, GQ], cosine[:, None], sine[:, None]).astype(jnp.bfloat16)
    values_new = mixed[:, :, GQ + 1].astype(jnp.bfloat16)

    def advance(carry, owner_index):
        partial_now = owner_partial(owner_index, queries, keys_new, values_new, cache_keys, cache_values, group_lengths, group_owner, group_start, listed_rows)
        return (combine(carry, partial_now), None)
    initial = (jnp.full((R, KVH, GQ), masked_score, jnp.float32), jnp.zeros((R, KVH, GQ), jnp.float32), jnp.zeros((R, KVH, GQ, HD), jnp.float32))
    (peaks, totals, numerator), _ = lax.scan(advance, initial, jnp.arange(N_GROUPS).astype(jnp.int32))
    heads_out = (numerator / totals[..., None]).astype(jnp.bfloat16).reshape(R, KVH * GQ * HD)
    attended = jnp.dot(heads_out, out_weight, preferred_element_type=jnp.float32)
    resid = hidden_rows.astype(jnp.float32) + attended
    squares = lax.optimization_barrier(jnp.sum(resid * resid, axis=1))
    normed = (resid * lax.rsqrt(squares / D + epsilon)[:, None] * norm_gain[None, :]).astype(jnp.bfloat16)
    next_qkv = jnp.dot(normed, next_weight, preferred_element_type=jnp.float32).astype(jnp.bfloat16)
    return (resid.astype(jnp.bfloat16), next_qkv)
```

```python
import functools

import jax
import jax.numpy as jnp
from jax import lax
from jax.experimental import pallas as pl
from jax.experimental.pallas import tpu as pltpu
from jax.sharding import PartitionSpec as P

HD = 128
GQ = 8
BLK = 128
MESH = pl.DeviceIdType.MESH
theta_base = 500000.0
epsilon = 1e-05
masked_score = -1e30
NEVER = 1 << 30
LIMIT = 56 * 1024 * 1024


def angles(positions, half_dim):
    freq = theta_base ** (-(jnp.arange(half_dim).astype(jnp.float32) * 2.0 / (2 * half_dim)))
    phase = positions.astype(jnp.float32)[:, None] * freq[None, :]
    return (jnp.cos(phase), jnp.sin(phase))


def full_angles(positions):
    cosine, sine = angles(positions, HD // 2)
    return (
        jnp.concatenate([cosine, cosine], axis=1),
        jnp.concatenate([-sine, sine], axis=1),
    )


def round_up(value, unit):
    return (value + unit - 1) // unit * unit


def remote(src, dst, send_sem, recv_sem, axis, index):
    return pltpu.make_async_remote_copy(
        src_ref=src,
        dst_ref=dst,
        send_sem=send_sem,
        recv_sem=recv_sem,
        device_id={axis: index},
        device_id_type=MESH,
    )


def sibling_of(me):
    return me + 1 - 2 * (me % 2)


def across_of(me):
    return me + 2 - 4 * ((me // 2) % 2)


def greet_pairs(count):
    me = lax.axis_index("groups")
    chips = count // 2
    barrier = pltpu.get_barrier_semaphore()
    pl.semaphore_signal(
        barrier, inc=1, device_id={"groups": sibling_of(me)}, device_id_type=MESH
    )

    @pl.loop(1, chips)
    def _(k):
        other = ((me // 2 + k) % chips) * 2 + me % 2
        pl.semaphore_signal(barrier, inc=1, device_id={"groups": other}, device_id_type=MESH)

    pl.semaphore_wait(barrier, chips)


def gather_chunks(count, out, sems):
    send_a, recv_a, send_b, recv_b, send_c, recv_c = sems
    me = lax.axis_index("groups")
    rows = count // 4
    mine = me // 4
    lane = me % 4
    lane_across = across_of(me) % 4
    lane_sibling = sibling_of(me) % 4
    lane_diagonal = 3 - lane

    def along(k):
        place = (mine + k) % rows
        return remote(
            out.at[me], out.at[me], send_a.at[k], recv_a.at[mine], "groups", place * 4 + lane
        )

    def along_in(k):
        place = (mine + k) % rows
        slot = place * 4 + lane
        return remote(out.at[slot], out.at[slot], send_a.at[k], recv_a.at[place], "groups", slot)

    def across(place, at_lane):
        slot = place * 4 + at_lane
        return remote(
            out.at[slot],
            out.at[slot],
            send_b.at[place],
            recv_b.at[place],
            "groups",
            across_of(me),
        )

    def sideways(place, at_lane, half):
        slot = place * 4 + at_lane
        return remote(
            out.at[slot],
            out.at[slot],
            send_c.at[half, place],
            recv_c.at[half, place],
            "groups",
            sibling_of(me),
        )

    @pl.loop(1, rows)
    def _(k):
        along(k).start()

    across(mine, lane).start()
    sideways(mine, lane, 0).start()

    @pl.loop(1, rows)
    def _(k):
        along_in(k).wait_recv()
        place = (mine + k) % rows
        across(place, lane).start()
        sideways(place, lane, 0).start()

    @pl.loop(0, rows)
    def _(k):
        place = (mine + k) % rows
        across(place, lane_across).wait_recv()
        sideways(place, lane_across, 1).start()

    @pl.loop(0, rows)
    def _(k):
        place = (mine + k) % rows
        sideways(place, lane_sibling, 0).wait_recv()
        sideways(place, lane_diagonal, 1).wait_recv()
        across(place, lane).wait_send()
        sideways(place, lane, 0).wait_send()
        sideways(place, lane_across, 1).wait_send()

    @pl.loop(1, rows)
    def _(k):
        along(k).wait_send()


def gather_sems(count):
    rows = count // 4
    return [pltpu.SemaphoreType.DMA((rows,))] * 4 + [pltpu.SemaphoreType.DMA((2, rows))] * 2


def pair_copy(count, src, dst, send_sem, recv_sem, k):
    me = lax.axis_index("groups")
    chips = count // 2
    chip = (me // 2 + k) % chips
    other = sibling_of(me)
    return remote(
        src.at[chip * 2 + other % 2], dst.at[chip], send_sem.at[chip], recv_sem.at[chip],
        "groups", other,
    )


def chip_copy(count, src, dst, send_sem, recv_sem, k):
    me = lax.axis_index("groups")
    chips = count // 2
    chip = (me // 2 + k) % chips
    return remote(
        src.at[chip], dst.at[me // 2], send_sem.at[chip], recv_sem.at[me // 2],
        "groups", chip * 2 + me % 2,
    )


def chip_copy_in(count, src, dst, send_sem, recv_sem, k):
    me = lax.axis_index("groups")
    chips = count // 2
    chip = (me // 2 + k) % chips
    return remote(
        src.at[chip], dst.at[chip], send_sem.at[chip], recv_sem.at[chip],
        "groups", chip * 2 + me % 2,
    )


def reduce_chunks(count, part, pair, out, into, total, sems):
    pair_send, pair_recv, chip_send, chip_recv = sems
    me = lax.axis_index("groups")
    chips = count // 2
    mine = me // 2

    @pl.loop(1, chips + 1)
    def _(k):
        pair_copy(count, part, pair, pair_send, pair_recv, k).start()

    @pl.loop(1, chips)
    def _(k):
        chip = (mine + k) % chips
        pair_copy(count, part, pair, pair_send, pair_recv, k).wait_recv()
        out[chip] = (part[chip * 2 + me % 2] + pair[chip]).astype(jnp.bfloat16)
        chip_copy(count, out, into, chip_send, chip_recv, k).start()

    pair_copy(count, part, pair, pair_send, pair_recv, chips).wait_recv()
    total[...] = part[me] + pair[mine]

    @pl.loop(1, chips)
    def _(k):
        chip = (mine + k) % chips
        chip_copy_in(count, out, into, chip_send, chip_recv, k).wait_recv()
        total[...] += into[chip].astype(jnp.float32)

    @pl.loop(1, chips + 1)
    def _(k):
        pair_copy(count, part, pair, pair_send, pair_recv, k).wait_send()

    @pl.loop(1, chips)
    def _(k):
        chip_copy(count, out, into, chip_send, chip_recv, k).wait_send()


def reduce_scratch(count, rows, columns):
    chips = count // 2
    return [
        pltpu.VMEM((count, rows, columns), jnp.float32),
        pltpu.VMEM((chips, rows, columns), jnp.float32),
        pltpu.VMEM((chips, rows, columns), jnp.bfloat16),
        pltpu.VMEM((chips, rows, columns), jnp.bfloat16),
        pltpu.VMEM((rows, columns), jnp.float32),
    ] + [pltpu.SemaphoreType.DMA((chips,))] * 4


def project_kernel(
    count, hidden, weight, cosine, sine, queries, news,
    part, pair, out, into, total, ps, pr, cs, cr, *gather,
):
    me = lax.axis_index("groups")
    rows, wide = part.shape[1:]
    heads = weight.shape[1] // wide
    tile = 2 * HD
    per = wide // tile

    @pl.loop(0, heads * per)
    def _(t):
        head = t // per
        here = pl.ds(pl.multiple_of(t * tile, tile), tile)
        there = pl.ds(pl.multiple_of((t % per) * tile, tile), tile)
        piece = jnp.dot(hidden[...], weight[:, here], preferred_element_type=jnp.float32)
        for block in range(count // heads):
            part[block * heads + head, :, there] = piece[block * rows : (block + 1) * rows]

    greet_pairs(count)
    reduce_chunks(count, part, pair, out, into, total, (ps, pr, cs, cr))
    for index in range(GQ + 1):
        vector = total[:, index * HD : (index + 1) * HD]
        turned = vector * cosine[...] + pltpu.roll(vector, HD // 2, 1) * sine[...]
        if index < GQ:
            queries[me, :, index * HD : (index + 1) * HD] = turned.astype(jnp.bfloat16)
        else:
            news[:, :HD] = turned.astype(jnp.bfloat16)
    news[:, HD:] = total[:, (GQ + 1) * HD :].astype(jnp.bfloat16)
    gather_chunks(count, queries, gather)


def attend_kernel(
    queries, cache_keys, cache_values, cosine, sine, news, key_pos, listed, numer, stats,
    keys, values, mask,
):
    capacity = cache_keys.shape[0]
    fresh = news.shape[0]
    blocks, rows = queries.shape[0], queries.shape[2]
    span = keys.shape[0]
    for block in range(capacity // BLK):
        here = slice(block * BLK, (block + 1) * BLK)
        vector = cache_keys[here, :].astype(jnp.float32)
        turned = (
            vector * cosine[block : block + 1, :]
            + pltpu.roll(vector, HD // 2, 1) * sine[block : block + 1, :]
        )
        keys[here, :] = turned.astype(jnp.bfloat16)
    values[:, HD:] = jnp.ones((span, HD), jnp.bfloat16)
    values[:capacity, :HD] = cache_values[...]
    keys[capacity : capacity + fresh, :] = news[:, :HD]
    values[capacity : capacity + fresh, :HD] = news[:, HD:]
    if span > capacity + fresh:
        rest = span - capacity - fresh
        keys[capacity + fresh :, :] = jnp.zeros((rest, HD), jnp.bfloat16)
        values[capacity + fresh :, :HD] = jnp.zeros((rest, HD), jnp.bfloat16)
    mask[...] = jnp.where(key_pos[0] <= listed[...], 0.0, masked_score)
    scale = HD ** (-0.5)
    lanes = lax.broadcasted_iota(jnp.int32, (blocks * rows, HD), 1)
    summary = jnp.zeros((blocks * rows, HD), jnp.float32)
    for index in range(GQ):
        here = slice(index * HD, (index + 1) * HD)
        query = queries[:, 0, :, here].reshape(blocks * rows, HD)
        scores = lax.dot_general(
            query, keys[...], (((1,), (1,)), ((), ())), preferred_element_type=jnp.float32
        )
        scores = scores + mask[...]
        peak = jnp.max(scores, axis=1, keepdims=True)
        weights = jnp.exp((scores - jnp.maximum(peak, -1e25)) * scale).astype(jnp.bfloat16)
        both = jnp.dot(weights, values[...], preferred_element_type=jnp.float32)
        totals = both[:, HD:]
        some = totals > 0.0
        safe = jnp.where(some, totals, 1.0)
        numer[:, 0, :, here] = (both[:, :HD] / safe).reshape(blocks, rows, HD)
        level = jnp.where(some, peak * scale + jnp.log(safe), masked_score)
        summary = jnp.where(lanes == index, level, summary)
    stats[:, 0] = summary.reshape(blocks, rows, HD)


def combine_kernel(
    count, numer, stats, heads_out,
    pair, pair_level, out, out_level, into, into_level, total, total_level,
    ps, pr, pls, plr, cs, cr, cls, clr, *gather,
):
    me = lax.axis_index("groups")
    chips = count // 2
    mine = me // 2
    greet_pairs(count)

    @pl.loop(1, chips + 1)
    def _(k):
        pair_copy(count, stats, pair_level, pls, plr, k).start()
        pair_copy(count, numer, pair, ps, pr, k).start()

    def merged(k, chip):
        slot = chip * 2 + me % 2
        pair_copy(count, stats, pair_level, pls, plr, k).wait_recv()
        pair_copy(count, numer, pair, ps, pr, k).wait_recv()
        one, two = stats[slot], pair_level[chip]
        top = jnp.maximum(one, two)
        one, two = jnp.exp(one - top), jnp.exp(two - top)
        both = one + two
        one, two = one / both, two / both
        parts = []
        for index in range(GQ):
            here = slice(index * HD, (index + 1) * HD)
            parts.append(
                numer[slot, :, here] * one[:, index : index + 1]
                + pair[chip, :, here] * two[:, index : index + 1]
            )
        return parts, top + jnp.log(both)

    @pl.loop(1, chips)
    def _(k):
        chip = (mine + k) % chips
        parts, level = merged(k, chip)
        out_level[chip] = level
        chip_copy(count, out_level, into_level, cls, clr, k).start()
        for index in range(GQ):
            out[chip, :, index * HD : (index + 1) * HD] = parts[index].astype(jnp.bfloat16)
        chip_copy(count, out, into, cs, cr, k).start()

    parts, level = merged(chips, mine)
    for index in range(GQ):
        total[:, index * HD : (index + 1) * HD] = parts[index]
    total_level[...] = level

    @pl.loop(1, chips)
    def _(k):
        chip = (mine + k) % chips
        chip_copy_in(count, out_level, into_level, cls, clr, k).wait_recv()
        chip_copy_in(count, out, into, cs, cr, k).wait_recv()
        one, two = total_level[...], into_level[chip]
        top = jnp.maximum(one, two)
        one, two = jnp.exp(one - top), jnp.exp(two - top)
        both = one + two
        total_level[...] = top + jnp.log(both)
        one, two = one / both, two / both
        for index in range(GQ):
            here = slice(index * HD, (index + 1) * HD)
            total[:, here] = (
                total[:, here] * one[:, index : index + 1]
                + into[chip, :, here].astype(jnp.float32) * two[:, index : index + 1]
            )

    heads_out[me] = total[...].astype(jnp.bfloat16)
    gather_chunks(count, heads_out, gather)

    @pl.loop(1, chips + 1)
    def _(k):
        pair_copy(count, stats, pair_level, pls, plr, k).wait_send()
        pair_copy(count, numer, pair, ps, pr, k).wait_send()

    @pl.loop(1, chips)
    def _(k):
        chip_copy(count, out_level, into_level, cls, clr, k).wait_send()
        chip_copy(count, out, into, cs, cr, k).wait_send()


def output_kernel(
    count, splits, wanted, heads_out, hidden, gain, out_weight, next_weight, hidden_out, next_out,
    out_held, next_held, load_sem, terms, term_send, term_recv, square, square_send, square_recv,
    scaled, left, part, pair, out, into, total, ps, pr, cs, cr,
):
    me = lax.axis_index("groups")
    my_split = lax.axis_index("heads")
    chunk = heads_out.shape[1]
    height = hidden.shape[0]
    kv_local = out_held.shape[0] // heads_out.shape[2]
    depth = heads_out.shape[2]
    loads = [
        pltpu.make_async_copy(out_weight, out_held, load_sem.at[0]),
        pltpu.make_async_copy(next_weight, next_held, load_sem.at[1]),
    ]
    for load in loads:
        load.start()

    barrier = pltpu.get_barrier_semaphore()

    @pl.loop(1, count)
    def _(k):
        pl.semaphore_signal(
            barrier, inc=1, device_id={"groups": (me + k) % count}, device_id_type=MESH
        )

    @pl.loop(1, splits)
    def _(k):
        pl.semaphore_signal(
            barrier, inc=1, device_id={"heads": (my_split + k) % splits}, device_id_type=MESH
        )

    loads[0].wait()
    term = jnp.zeros((height, hidden.shape[1]), jnp.float32)
    for head in range(kv_local):
        block = heads_out[...].reshape(count // kv_local, kv_local, chunk, depth)[:, head]
        term += jnp.dot(
            block.reshape(height, depth),
            out_held[head * depth : (head + 1) * depth, :],
            preferred_element_type=jnp.float32,
        )
    terms[my_split] = term.astype(jnp.bfloat16)
    pl.semaphore_wait(barrier, count - 1 + splits - 1)

    def share(k):
        return remote(
            terms.at[my_split], terms.at[my_split], term_send.at[k], term_recv.at[my_split],
            "heads", (my_split + k) % splits,
        )

    def share_in(k):
        other = (my_split + k) % splits
        return remote(
            terms.at[other], terms.at[other], term_send.at[k], term_recv.at[other], "heads", other
        )

    @pl.loop(1, splits)
    def _(k):
        share(k).start()

    @pl.loop(1, splits)
    def _(k):
        share_in(k).wait_recv()

    attended = terms[0].astype(jnp.float32)
    for index in range(1, splits):
        attended += terms[index].astype(jnp.float32)
    resid = hidden[...].astype(jnp.float32) + attended
    hidden_out[...] = resid.astype(jnp.bfloat16)
    column = jnp.sum(resid * resid, axis=1, keepdims=True)
    diagonal = lax.broadcasted_iota(jnp.int32, (height, height), 0) == lax.broadcasted_iota(
        jnp.int32, (height, height), 1
    )
    line = jnp.sum(jnp.where(diagonal, column, 0.0), axis=0, keepdims=True)
    square[me] = jnp.broadcast_to(line, square.shape[1:])

    def spread(k):
        return remote(
            square.at[me], square.at[me], square_send.at[k], square_recv.at[me],
            "groups", (me + k) % count,
        )

    def spread_in(k):
        other = (me + k) % count
        return remote(
            square.at[other], square.at[other], square_send.at[k], square_recv.at[other],
            "groups", other,
        )

    @pl.loop(1, count)
    def _(k):
        spread(k).start()

    scaled[...] = resid * gain[...]

    @pl.loop(1, count)
    def _(k):
        spread_in(k).wait_recv()

    line = jnp.sum(square[...], axis=0)[0:1, :]
    squares = jnp.sum(jnp.where(diagonal, line, 0.0), axis=1, keepdims=True)
    width = hidden.shape[1] * count
    scaled[...] = scaled[...] * lax.rsqrt(squares / width + epsilon)

    held_rows = left.shape[1]
    own_rows = wanted
    left[...] = jnp.zeros_like(left)
    for index in range(count):
        first = (index // kv_local) * chunk + (index % kv_local) * own_rows
        left[index, :own_rows, :] = scaled[first : first + own_rows, :]
    lhs = left[...].reshape(count * held_rows, hidden.shape[1]).astype(jnp.bfloat16)
    loads[1].wait()
    tile = 2 * HD

    @pl.loop(0, next_held.shape[1] // tile)
    def _(t):
        here = pl.ds(pl.multiple_of(t * tile, tile), tile)
        piece = jnp.dot(lhs, next_held[:, here], preferred_element_type=jnp.float32)
        part[:, :, here] = piece.reshape(count, held_rows, tile)

    reduce_chunks(count, part, pair, out, into, total, (ps, pr, cs, cr))
    next_out[...] = total[...].astype(jnp.bfloat16)

    @pl.loop(1, splits)
    def _(k):
        share(k).wait_send()

    @pl.loop(1, count)
    def _(k):
        spread(k).wait_send()


def layout(
    owner_index, group_lengths, group_owner, group_start, listed_rows, cap_blocks, block_rows
):
    block_len = group_lengths // block_rows
    holder = (group_owner == owner_index).astype(jnp.int32)
    held_blocks = holder * block_len
    offset = jnp.cumsum(held_blocks) - held_blocks
    block_ids = jnp.arange(cap_blocks)[:, None]
    member = (
        (holder[None, :] == 1)
        & (block_ids >= offset[None, :])
        & (block_ids < offset[None, :] + block_len[None, :])
    ).astype(jnp.int32)
    shift_blk = jnp.sum(member * group_start[None, :], axis=1)
    begin_blk = jnp.sum(
        member * (group_start[None, :] + (block_ids - offset[None, :]) * block_rows), axis=1
    )
    live_blk = jnp.sum(member, axis=1) > 0
    inside = jnp.arange(block_rows)[None, :]
    key_pos = (begin_blk[:, None] + inside).reshape(-1)
    listed_hit = jnp.any(key_pos[:, None] == listed_rows[None, :], axis=1)
    key_live = jnp.repeat(live_blk, block_rows) & jnp.logical_not(listed_hit)
    return (jnp.where(key_live, key_pos, NEVER), shift_blk)


VMEM = pl.BlockSpec(memory_space=pltpu.VMEM)
ANY = pl.BlockSpec(memory_space=pl.ANY)


def on_device(
    count,
    splits,
    hidden_rows,
    qkv_weight,
    out_weight,
    norm_gain,
    next_weight,
    cache_keys,
    cache_values,
    group_lengths,
    group_owner,
    group_start,
    listed_rows,
):
    me = lax.axis_index("groups")
    row_count, model_part = hidden_rows.shape
    depth = GQ * HD
    kv_local = out_weight.shape[0] // depth
    wide = (GQ + 2) * HD
    blocks = count // kv_local
    own = row_count // blocks
    chunk = round_up(own, 16)
    height = blocks * chunk
    capacity = cache_keys.shape[0]

    def padded(array):
        if chunk == own:
            return array
        array = array.reshape((blocks, own) + array.shape[1:])
        fill = [(0, 0), (0, chunk - own)] + [(0, 0)] * (array.ndim - 2)
        return jnp.pad(array, fill).reshape((height,) + array.shape[2:])

    hidden = padded(hidden_rows)
    listed = padded(listed_rows)
    own_pos = lax.dynamic_slice_in_dim(listed, (me // kv_local) * chunk, chunk)
    own_cos, own_sin = full_angles(own_pos)
    queries, news = pl.pallas_call(
        functools.partial(project_kernel, count),
        out_shape=(
            jax.ShapeDtypeStruct((count, chunk, depth), jnp.bfloat16),
            jax.ShapeDtypeStruct((chunk, 2 * HD), jnp.bfloat16),
        ),
        in_specs=[VMEM] * 4,
        out_specs=(VMEM, VMEM),
        scratch_shapes=reduce_scratch(count, chunk, wide) + gather_sems(count),
        compiler_params=pltpu.CompilerParams(
            collective_id=0, has_side_effects=True, vmem_limit_bytes=LIMIT
        ),
        name="project",
    )(hidden, qkv_weight, own_cos, own_sin)

    key_pos, key_shift = layout(
        me, group_lengths, group_owner, group_start, listed_rows, capacity // BLK, BLK
    )
    store_cos, store_sin = full_angles(key_shift)
    span = round_up(capacity + chunk, BLK)
    fresh_pos = jnp.where(jnp.arange(chunk) < own, own_pos, NEVER)
    fresh_pos = jnp.where(
        jnp.arange(kv_local)[:, None] == me % kv_local, fresh_pos[None, :], NEVER
    )
    all_pos = jnp.concatenate(
        [
            jnp.broadcast_to(key_pos[None, :], (kv_local, capacity)),
            fresh_pos,
            jnp.full((kv_local, span - capacity - chunk), NEVER, jnp.int32),
        ],
        axis=1,
    )[:, None, :]
    steady = lambda shape: pl.BlockSpec(shape, lambda h: (0,) * len(shape))
    numer, stats = pl.pallas_call(
        attend_kernel,
        grid=(kv_local,),
        out_shape=(
            jax.ShapeDtypeStruct((blocks, kv_local, chunk, depth), jnp.float32),
            jax.ShapeDtypeStruct((blocks, kv_local, chunk, HD), jnp.float32),
        ),
        in_specs=[
            pl.BlockSpec((blocks, 1, chunk, depth), lambda h: (0, h, 0, 0)),
            pl.BlockSpec((capacity, HD), lambda h: (0, h)),
            pl.BlockSpec((capacity, HD), lambda h: (0, h)),
            steady(store_cos.shape),
            steady(store_sin.shape),
            steady((chunk, 2 * HD)),
            pl.BlockSpec((1, 1, span), lambda h: (h, 0, 0)),
            steady((height, 1)),
        ],
        out_specs=(
            pl.BlockSpec((blocks, 1, chunk, depth), lambda h: (0, h, 0, 0)),
            pl.BlockSpec((blocks, 1, chunk, HD), lambda h: (0, h, 0, 0)),
        ),
        scratch_shapes=[
            pltpu.VMEM((span, HD), jnp.bfloat16),
            pltpu.VMEM((span, 2 * HD), jnp.bfloat16),
            pltpu.VMEM((height, span), jnp.float32),
        ],
        compiler_params=pltpu.CompilerParams(vmem_limit_bytes=LIMIT),
        name="attend",
    )(
        queries.reshape(blocks, kv_local, chunk, depth),
        cache_keys,
        cache_values,
        store_cos,
        store_sin,
        news,
        all_pos,
        listed[:, None],
    )

    chips = count // 2
    heads_out = pl.pallas_call(
        functools.partial(combine_kernel, count),
        out_shape=jax.ShapeDtypeStruct((count, chunk, depth), jnp.bfloat16),
        in_specs=[VMEM] * 2,
        out_specs=VMEM,
        scratch_shapes=[
            pltpu.VMEM((chips, chunk, depth), jnp.float32),
            pltpu.VMEM((chips, chunk, HD), jnp.float32),
            pltpu.VMEM((chips, chunk, depth), jnp.bfloat16),
            pltpu.VMEM((chips, chunk, HD), jnp.float32),
            pltpu.VMEM((chips, chunk, depth), jnp.bfloat16),
            pltpu.VMEM((chips, chunk, HD), jnp.float32),
            pltpu.VMEM((chunk, depth), jnp.float32),
            pltpu.VMEM((chunk, HD), jnp.float32),
        ]
        + [pltpu.SemaphoreType.DMA((chips,))] * 8
        + gather_sems(count),
        compiler_params=pltpu.CompilerParams(
            collective_id=1, has_side_effects=True, vmem_limit_bytes=LIMIT
        ),
        name="combine",
    )(numer.reshape(count, chunk, depth), stats.reshape(count, chunk, HD))

    held = round_up(row_count // count, 16)
    next_wide = next_weight.shape[1]
    hidden_out, next_out = pl.pallas_call(
        functools.partial(output_kernel, count, splits, row_count // count),
        out_shape=(
            jax.ShapeDtypeStruct((height, model_part), jnp.bfloat16),
            jax.ShapeDtypeStruct((held, next_wide), jnp.bfloat16),
        ),
        in_specs=[VMEM, VMEM, VMEM, ANY, ANY],
        out_specs=(VMEM, VMEM),
        scratch_shapes=[
            pltpu.VMEM(out_weight.shape, jnp.bfloat16),
            pltpu.VMEM(next_weight.shape, jnp.bfloat16),
            pltpu.SemaphoreType.DMA((2,)),
            pltpu.VMEM((splits, height, model_part), jnp.bfloat16),
            pltpu.SemaphoreType.DMA((splits,)),
            pltpu.SemaphoreType.DMA((splits,)),
            pltpu.VMEM((count, 8, height), jnp.float32),
            pltpu.SemaphoreType.DMA((count,)),
            pltpu.SemaphoreType.DMA((count,)),
            pltpu.VMEM((height, model_part), jnp.float32),
            pltpu.VMEM((count, held, model_part), jnp.float32),
        ]
        + reduce_scratch(count, held, next_wide),
        compiler_params=pltpu.CompilerParams(
            collective_id=2, has_side_effects=True, vmem_limit_bytes=LIMIT
        ),
        name="output",
    )(heads_out, hidden, norm_gain[None, :], out_weight, next_weight)
    if chunk != own:
        hidden_out = hidden_out.reshape(blocks, chunk, model_part)[:, :own]
        hidden_out = hidden_out.reshape(row_count, model_part)
    return (hidden_out, next_out[: row_count // count])


def solution(mesh):
    in_specs = (
        P(None, "groups"),
        P("groups", "heads"),
        P("heads", "groups"),
        P("groups"),
        P("groups", "heads"),
        P("groups", "heads"),
        P("groups", "heads"),
        P(),
        P(),
        P(),
        P(),
    )
    out_specs = (P(None, "groups"), P("groups", "heads"))
    return jax.shard_map(
        functools.partial(on_device, mesh.shape["groups"], mesh.shape["heads"]),
        mesh=mesh,
        in_specs=in_specs,
        out_specs=out_specs,
        check_vma=False,
    )
```

```python
import functools

import jax
import jax.numpy as jnp
from jax import lax
from jax.experimental import pallas as pl
from jax.experimental.pallas import tpu as pltpu
from jax.sharding import PartitionSpec as P

HD = 128
GQ = 8
BLK = 128
MESH = pl.DeviceIdType.MESH
theta_base = 500000.0
epsilon = 1e-05
masked_score = -1e30
NEVER = 1 << 30
LIMIT = 56 * 1024 * 1024


def angles(positions, half_dim):
    freq = theta_base ** (-(jnp.arange(half_dim).astype(jnp.float32) * 2.0 / (2 * half_dim)))
    phase = positions.astype(jnp.float32)[:, None] * freq[None, :]
    return (jnp.cos(phase), jnp.sin(phase))


def full_angles(positions):
    cosine, sine = angles(positions, HD // 2)
    return (
        jnp.concatenate([cosine, cosine], axis=1),
        jnp.concatenate([-sine, sine], axis=1),
    )


def round_up(value, unit):
    return (value + unit - 1) // unit * unit


def remote(src, dst, send_sem, recv_sem, axis, index):
    return pltpu.make_async_remote_copy(
        src_ref=src,
        dst_ref=dst,
        send_sem=send_sem,
        recv_sem=recv_sem,
        device_id={axis: index},
        device_id_type=MESH,
    )


def sibling_of(me):
    return me + 1 - 2 * (me % 2)


def across_of(me):
    return me + 2 - 4 * ((me // 2) % 2)


def greet(count):
    me = lax.axis_index("groups")
    rows = count // 4
    barrier = pltpu.get_barrier_semaphore()
    for other in (sibling_of(me), across_of(me)):
        pl.semaphore_signal(barrier, inc=1, device_id={"groups": other}, device_id_type=MESH)

    @pl.loop(1, rows)
    def _(k):
        other = ((me // 4 + k) % rows) * 4 + me % 4
        pl.semaphore_signal(barrier, inc=1, device_id={"groups": other}, device_id_type=MESH)

    pl.semaphore_wait(barrier, rows + 1)


def gather_chunks(count, out, sems):
    send_a, recv_a, send_b, recv_b, send_c, recv_c = sems
    me = lax.axis_index("groups")
    rows = count // 4
    mine = me // 4
    lane = me % 4
    lane_across = across_of(me) % 4
    lane_sibling = sibling_of(me) % 4
    lane_diagonal = 3 - lane

    def along(k):
        place = (mine + k) % rows
        return remote(
            out.at[me], out.at[me], send_a.at[k], recv_a.at[mine], "groups", place * 4 + lane
        )

    def along_in(k):
        place = (mine + k) % rows
        slot = place * 4 + lane
        return remote(out.at[slot], out.at[slot], send_a.at[k], recv_a.at[place], "groups", slot)

    def across(place, at_lane):
        slot = place * 4 + at_lane
        return remote(
            out.at[slot],
            out.at[slot],
            send_b.at[place],
            recv_b.at[place],
            "groups",
            across_of(me),
        )

    def sideways(place, at_lane, half):
        slot = place * 4 + at_lane
        return remote(
            out.at[slot],
            out.at[slot],
            send_c.at[half, place],
            recv_c.at[half, place],
            "groups",
            sibling_of(me),
        )

    @pl.loop(1, rows)
    def _(k):
        along(k).start()

    across(mine, lane).start()
    sideways(mine, lane, 0).start()

    @pl.loop(1, rows)
    def _(k):
        along_in(k).wait_recv()
        place = (mine + k) % rows
        across(place, lane).start()
        sideways(place, lane, 0).start()

    @pl.loop(0, rows)
    def _(k):
        place = (mine + k) % rows
        across(place, lane_across).wait_recv()
        sideways(place, lane_across, 1).start()

    @pl.loop(0, rows)
    def _(k):
        place = (mine + k) % rows
        sideways(place, lane_sibling, 0).wait_recv()
        sideways(place, lane_diagonal, 1).wait_recv()
        across(place, lane).wait_send()
        sideways(place, lane, 0).wait_send()
        sideways(place, lane_across, 1).wait_send()

    @pl.loop(1, rows)
    def _(k):
        along(k).wait_send()


def gather_sems(count):
    rows = count // 4
    return [pltpu.SemaphoreType.DMA((rows,))] * 4 + [pltpu.SemaphoreType.DMA((2, rows))] * 2


def whole_chunk(part, chip, core):
    return part.at[chip * 2 + core]


def half_chunk(part, chip, core):
    half = part.shape[2] // 2
    return part.at[chip, :, pl.ds(pl.multiple_of(core * half, HD), half)]


def reduce_chunks(count, fields, merge, view):
    me = lax.axis_index("groups")
    rows = count // 4
    core, side, mine = me % 2, (me // 2) % 2, me // 4
    sibling, opposite = sibling_of(me), across_of(me)

    def pair_copy(field, chip):
        part, pair, sems = field[0], field[1], field[6]
        return remote(
            view(part, chip, sibling % 2), pair.at[chip], sems[0].at[chip], sems[1].at[chip],
            "groups", sibling,
        )

    def across(field, place):
        sems = field[6]
        return remote(
            field[2].at[place], field[3].at[place], sems[2].at[place], sems[3].at[place],
            "groups", opposite,
        )

    def along(field, place, slot):
        sems = field[6]
        return remote(
            field[4].at[place], field[5].at[slot], sems[4].at[place], sems[5].at[slot],
            "groups", place * 4 + me % 4,
        )

    def on_chip(chip):
        for field in fields:
            pair_copy(field, chip).wait_recv()
        return merge(
            [view(field[0], chip, core)[...] for field in fields],
            [field[1][chip] for field in fields],
        )

    for wanted in (1 - side, side):

        @pl.loop(1, rows + 1)
        def _(k):
            for field in fields:
                pair_copy(field, ((mine + k) % rows) * 2 + wanted).start()

    @pl.loop(1, rows + 1)
    def _(k):
        place = (mine + k) % rows
        for field, value in zip(fields, on_chip(place * 2 + 1 - side)):
            field[2][place] = value.astype(field[2].dtype)
            across(field, place).start()

    def on_row(place):
        value = on_chip(place * 2 + side)
        for field in fields:
            across(field, place).wait_recv()
        return merge(value, [field[3][place].astype(jnp.float32) for field in fields])

    @pl.loop(1, rows)
    def _(k):
        place = (mine + k) % rows
        for field, value in zip(fields, on_row(place)):
            field[4][place] = value.astype(field[4].dtype)
            along(field, place, mine).start()

    value = on_row(mine)
    for k in range(1, rows):
        place = (mine + k) % rows
        for field in fields:
            along(field, place, place).wait_recv()
        value = merge(value, [field[5][place].astype(jnp.float32) for field in fields])

    @pl.loop(0, count // 2)
    def _(chip):
        for field in fields:
            pair_copy(field, chip).wait_send()

    @pl.loop(0, rows)
    def _(place):
        for field in fields:
            across(field, place).wait_send()

    @pl.loop(1, rows)
    def _(k):
        for field in fields:
            along(field, (mine + k) % rows, mine).wait_send()

    return value


def added(one, two):
    return [one[0] + two[0]]


def merged(one, two):
    top = jnp.maximum(one[1], two[1])
    first, second = jnp.exp(one[1] - top), jnp.exp(two[1] - top)
    both = first + second
    first, second = first / both, second / both
    parts = []
    for index in range(GQ):
        here = slice(index * HD, (index + 1) * HD)
        parts.append(
            one[0][:, here] * first[:, index : index + 1]
            + two[0][:, here] * second[:, index : index + 1]
        )
    return [jnp.concatenate(parts, axis=1), top + jnp.log(both)]


def reduce_scratch(count, rows, columns, dtype):
    place = pltpu.VMEM((count // 4, rows, columns), dtype)
    return [pltpu.VMEM((count // 2, rows, columns), jnp.float32), place, place, place, place] + [
        pltpu.SemaphoreType.DMA((count // 2,))
    ] * 2 + [pltpu.SemaphoreType.DMA((count // 4,))] * 4


FIELD = 11


def field_of(part, scratch):
    return (part, *scratch[:5], scratch[5:FIELD])


def project_kernel(
    count, hidden, weight, cosine, sine, queries, news,
    part, *scratch,
):
    me = lax.axis_index("groups")
    rows, wide = part.shape[1:]
    heads = weight.shape[1] // wide
    tile = 2 * HD
    per = wide // tile

    @pl.loop(0, heads * per)
    def _(t):
        head = t // per
        here = pl.ds(pl.multiple_of(t * tile, tile), tile)
        there = pl.ds(pl.multiple_of((t % per) * tile, tile), tile)
        piece = jnp.dot(hidden[...], weight[:, here], preferred_element_type=jnp.float32)
        for block in range(count // heads):
            part[block * heads + head, :, there] = piece[block * rows : (block + 1) * rows]

    greet(count)
    (total,) = reduce_chunks(count, [field_of(part, scratch)], added, whole_chunk)
    for index in range(GQ + 1):
        vector = total[:, index * HD : (index + 1) * HD]
        turned = vector * cosine[...] + pltpu.roll(vector, HD // 2, 1) * sine[...]
        if index < GQ:
            queries[me, :, index * HD : (index + 1) * HD] = turned.astype(jnp.bfloat16)
        else:
            news[:, :HD] = turned.astype(jnp.bfloat16)
    news[:, HD:] = total[:, (GQ + 1) * HD :].astype(jnp.bfloat16)
    gather_chunks(count, queries, scratch[FIELD:])


def attend_kernel(
    queries, cache_keys, cache_values, cosine, sine, news, key_pos, listed, numer, stats,
    keys, values, mask,
):
    capacity = cache_keys.shape[0]
    fresh = news.shape[0]
    blocks, rows = queries.shape[0], queries.shape[2]
    span = keys.shape[0]
    for block in range(capacity // BLK):
        here = slice(block * BLK, (block + 1) * BLK)
        vector = cache_keys[here, :].astype(jnp.float32)
        turned = (
            vector * cosine[block : block + 1, :]
            + pltpu.roll(vector, HD // 2, 1) * sine[block : block + 1, :]
        )
        keys[here, :] = turned.astype(jnp.bfloat16)
    values[:, HD:] = jnp.ones((span, HD), jnp.bfloat16)
    values[:capacity, :HD] = cache_values[...]
    keys[capacity : capacity + fresh, :] = news[:, :HD]
    values[capacity : capacity + fresh, :HD] = news[:, HD:]
    if span > capacity + fresh:
        rest = span - capacity - fresh
        keys[capacity + fresh :, :] = jnp.zeros((rest, HD), jnp.bfloat16)
        values[capacity + fresh :, :HD] = jnp.zeros((rest, HD), jnp.bfloat16)
    mask[...] = jnp.where(key_pos[0] <= listed[...], 0.0, masked_score)
    scale = HD ** (-0.5)
    lanes = lax.broadcasted_iota(jnp.int32, (blocks * rows, HD), 1)
    summary = jnp.zeros((blocks * rows, HD), jnp.float32)
    for index in range(GQ):
        here = slice(index * HD, (index + 1) * HD)
        query = queries[:, 0, :, here].reshape(blocks * rows, HD)
        scores = lax.dot_general(
            query, keys[...], (((1,), (1,)), ((), ())), preferred_element_type=jnp.float32
        )
        scores = scores + mask[...]
        peak = jnp.max(scores, axis=1, keepdims=True)
        weights = jnp.exp((scores - jnp.maximum(peak, -1e25)) * scale).astype(jnp.bfloat16)
        both = jnp.dot(weights, values[...], preferred_element_type=jnp.float32)
        totals = both[:, HD:]
        some = totals > 0.0
        safe = jnp.where(some, totals, 1.0)
        numer[:, 0, :, here] = (both[:, :HD] / safe).reshape(blocks, rows, HD)
        level = jnp.where(some, peak * scale + jnp.log(safe), masked_score)
        summary = jnp.where(lanes == index, level, summary)
    stats[:, 0] = summary.reshape(blocks, rows, HD)


def combine_kernel(count, numer, stats, heads_out, *scratch):
    me = lax.axis_index("groups")
    greet(count)
    fields = [field_of(numer, scratch), field_of(stats, scratch[FIELD:])]
    total, _ = reduce_chunks(count, fields, merged, whole_chunk)
    heads_out[me] = total.astype(jnp.bfloat16)
    gather_chunks(count, heads_out, scratch[2 * FIELD :])


def output_kernel(
    count, splits, wanted, heads_out, hidden, gain, out_weight, next_weight, hidden_out, next_out,
    out_held, next_held, load_sem, terms, term_send, term_recv, square, square_send, square_recv,
    scaled, left, swap_out, swap_in, swap_sem, part, *scratch,
):
    me = lax.axis_index("groups")
    my_split = lax.axis_index("heads")
    chunk = heads_out.shape[1]
    height = hidden.shape[0]
    kv_local = out_held.shape[0] // heads_out.shape[2]
    depth = heads_out.shape[2]
    loads = [
        pltpu.make_async_copy(out_weight, out_held, load_sem.at[0]),
        pltpu.make_async_copy(next_weight, next_held, load_sem.at[1]),
    ]
    for load in loads:
        load.start()

    barrier = pltpu.get_barrier_semaphore()

    @pl.loop(1, count)
    def _(k):
        pl.semaphore_signal(
            barrier, inc=1, device_id={"groups": (me + k) % count}, device_id_type=MESH
        )

    @pl.loop(1, splits)
    def _(k):
        pl.semaphore_signal(
            barrier, inc=1, device_id={"heads": (my_split + k) % splits}, device_id_type=MESH
        )

    loads[0].wait()
    term = jnp.zeros((height, hidden.shape[1]), jnp.float32)
    for head in range(kv_local):
        block = heads_out[...].reshape(count // kv_local, kv_local, chunk, depth)[:, head]
        term += jnp.dot(
            block.reshape(height, depth),
            out_held[head * depth : (head + 1) * depth, :],
            preferred_element_type=jnp.float32,
        )
    terms[my_split] = term.astype(jnp.bfloat16)
    pl.semaphore_wait(barrier, count - 1 + splits - 1)

    def share(k):
        return remote(
            terms.at[my_split], terms.at[my_split], term_send.at[k], term_recv.at[my_split],
            "heads", (my_split + k) % splits,
        )

    def share_in(k):
        other = (my_split + k) % splits
        return remote(
            terms.at[other], terms.at[other], term_send.at[k], term_recv.at[other], "heads", other
        )

    @pl.loop(1, splits)
    def _(k):
        share(k).start()

    @pl.loop(1, splits)
    def _(k):
        share_in(k).wait_recv()

    attended = terms[0].astype(jnp.float32)
    for index in range(1, splits):
        attended += terms[index].astype(jnp.float32)
    resid = hidden[...].astype(jnp.float32) + attended
    hidden_out[...] = resid.astype(jnp.bfloat16)
    column = jnp.sum(resid * resid, axis=1, keepdims=True)
    diagonal = lax.broadcasted_iota(jnp.int32, (height, height), 0) == lax.broadcasted_iota(
        jnp.int32, (height, height), 1
    )
    line = jnp.sum(jnp.where(diagonal, column, 0.0), axis=0, keepdims=True)
    square[me] = jnp.broadcast_to(line, square.shape[1:])

    def spread(k):
        return remote(
            square.at[me], square.at[me], square_send.at[k], square_recv.at[me],
            "groups", (me + k) % count,
        )

    def spread_in(k):
        other = (me + k) % count
        return remote(
            square.at[other], square.at[other], square_send.at[k], square_recv.at[other],
            "groups", other,
        )

    @pl.loop(1, count)
    def _(k):
        spread(k).start()

    scaled[...] = resid * gain[...]

    @pl.loop(1, count)
    def _(k):
        spread_in(k).wait_recv()

    line = jnp.sum(square[...], axis=0)[0:1, :]
    squares = jnp.sum(jnp.where(diagonal, line, 0.0), axis=1, keepdims=True)
    width = hidden.shape[1] * count
    scaled[...] = scaled[...] * lax.rsqrt(squares / width + epsilon)

    held = left.shape[1]
    if 2 * wanted == held and count * wanted == height:
        lhs = scaled[...].astype(jnp.bfloat16)
    else:
        left[...] = jnp.zeros_like(left)
        for index in range(count):
            first = (index // kv_local) * chunk + (index % kv_local) * wanted
            there = (index % 2) * wanted
            left[index // 2, there : there + wanted, :] = scaled[first : first + wanted, :]
        lhs = left[...].reshape(count // 2 * held, hidden.shape[1]).astype(jnp.bfloat16)
    loads[1].wait()
    tile = 2 * HD

    @pl.loop(0, next_held.shape[1] // tile)
    def _(t):
        here = pl.ds(pl.multiple_of(t * tile, tile), tile)
        piece = jnp.dot(lhs, next_held[:, here], preferred_element_type=jnp.float32)
        part[:, :, here] = piece.reshape(count // 2, held, tile)

    (total,) = reduce_chunks(count, [field_of(part, scratch)], added, half_chunk)
    half = total.shape[1]
    core = me % 2
    first, second = total[:wanted], total[wanted : 2 * wanted]
    filler = [jnp.zeros((next_out.shape[0] - wanted, half), jnp.float32)]
    keep = jnp.concatenate([jnp.where(core == 0, first, second)] + filler, axis=0)
    give = jnp.concatenate([jnp.where(core == 0, second, first)] + filler, axis=0)
    swap_out[...] = give.astype(jnp.bfloat16)
    swap = remote(
        swap_out, swap_in, swap_sem.at[0], swap_sem.at[1], "groups", sibling_of(me)
    )
    swap.start()
    next_out[:, pl.ds(pl.multiple_of(core * half, HD), half)] = keep.astype(jnp.bfloat16)
    swap.wait_recv()
    next_out[:, pl.ds(pl.multiple_of((1 - core) * half, HD), half)] = swap_in[...]
    swap.wait_send()

    @pl.loop(1, splits)
    def _(k):
        share(k).wait_send()

    @pl.loop(1, count)
    def _(k):
        spread(k).wait_send()


def layout(
    owner_index, group_lengths, group_owner, group_start, listed_rows, cap_blocks, block_rows
):
    block_len = group_lengths // block_rows
    holder = (group_owner == owner_index).astype(jnp.int32)
    held_blocks = holder * block_len
    offset = jnp.cumsum(held_blocks) - held_blocks
    block_ids = jnp.arange(cap_blocks)[:, None]
    member = (
        (holder[None, :] == 1)
        & (block_ids >= offset[None, :])
        & (block_ids < offset[None, :] + block_len[None, :])
    ).astype(jnp.int32)
    shift_blk = jnp.sum(member * group_start[None, :], axis=1)
    begin_blk = jnp.sum(
        member * (group_start[None, :] + (block_ids - offset[None, :]) * block_rows), axis=1
    )
    live_blk = jnp.sum(member, axis=1) > 0
    inside = jnp.arange(block_rows)[None, :]
    key_pos = (begin_blk[:, None] + inside).reshape(-1)
    listed_hit = jnp.any(key_pos[:, None] == listed_rows[None, :], axis=1)
    key_live = jnp.repeat(live_blk, block_rows) & jnp.logical_not(listed_hit)
    return (jnp.where(key_live, key_pos, NEVER), shift_blk)


VMEM = pl.BlockSpec(memory_space=pltpu.VMEM)
ANY = pl.BlockSpec(memory_space=pl.ANY)


def on_device(
    count,
    splits,
    hidden_rows,
    qkv_weight,
    out_weight,
    norm_gain,
    next_weight,
    cache_keys,
    cache_values,
    group_lengths,
    group_owner,
    group_start,
    listed_rows,
):
    me = lax.axis_index("groups")
    row_count, model_part = hidden_rows.shape
    depth = GQ * HD
    kv_local = out_weight.shape[0] // depth
    wide = (GQ + 2) * HD
    blocks = count // kv_local
    own = row_count // blocks
    chunk = round_up(own, 16)
    height = blocks * chunk
    capacity = cache_keys.shape[0]

    def padded(array):
        if chunk == own:
            return array
        array = array.reshape((blocks, own) + array.shape[1:])
        fill = [(0, 0), (0, chunk - own)] + [(0, 0)] * (array.ndim - 2)
        return jnp.pad(array, fill).reshape((height,) + array.shape[2:])

    hidden = padded(hidden_rows)
    listed = padded(listed_rows)
    own_pos = lax.dynamic_slice_in_dim(listed, (me // kv_local) * chunk, chunk)
    own_cos, own_sin = full_angles(own_pos)
    queries, news = pl.pallas_call(
        functools.partial(project_kernel, count),
        out_shape=(
            jax.ShapeDtypeStruct((count, chunk, depth), jnp.bfloat16),
            jax.ShapeDtypeStruct((chunk, 2 * HD), jnp.bfloat16),
        ),
        in_specs=[VMEM] * 4,
        out_specs=(VMEM, VMEM),
        scratch_shapes=[pltpu.VMEM((count, chunk, wide), jnp.float32)]
        + reduce_scratch(count, chunk, wide, jnp.bfloat16)
        + gather_sems(count),
        compiler_params=pltpu.CompilerParams(
            collective_id=0, has_side_effects=True, vmem_limit_bytes=LIMIT
        ),
        name="project",
    )(hidden, qkv_weight, own_cos, own_sin)

    key_pos, key_shift = layout(
        me, group_lengths, group_owner, group_start, listed_rows, capacity // BLK, BLK
    )
    store_cos, store_sin = full_angles(key_shift)
    span = round_up(capacity + chunk, BLK)
    fresh_pos = jnp.where(jnp.arange(chunk) < own, own_pos, NEVER)
    fresh_pos = jnp.where(
        jnp.arange(kv_local)[:, None] == me % kv_local, fresh_pos[None, :], NEVER
    )
    all_pos = jnp.concatenate(
        [
            jnp.broadcast_to(key_pos[None, :], (kv_local, capacity)),
            fresh_pos,
            jnp.full((kv_local, span - capacity - chunk), NEVER, jnp.int32),
        ],
        axis=1,
    )[:, None, :]
    steady = lambda shape: pl.BlockSpec(shape, lambda h: (0,) * len(shape))
    numer, stats = pl.pallas_call(
        attend_kernel,
        grid=(kv_local,),
        out_shape=(
            jax.ShapeDtypeStruct((blocks, kv_local, chunk, depth), jnp.float32),
            jax.ShapeDtypeStruct((blocks, kv_local, chunk, HD), jnp.float32),
        ),
        in_specs=[
            pl.BlockSpec((blocks, 1, chunk, depth), lambda h: (0, h, 0, 0)),
            pl.BlockSpec((capacity, HD), lambda h: (0, h)),
            pl.BlockSpec((capacity, HD), lambda h: (0, h)),
            steady(store_cos.shape),
            steady(store_sin.shape),
            steady((chunk, 2 * HD)),
            pl.BlockSpec((1, 1, span), lambda h: (h, 0, 0)),
            steady((height, 1)),
        ],
        out_specs=(
            pl.BlockSpec((blocks, 1, chunk, depth), lambda h: (0, h, 0, 0)),
            pl.BlockSpec((blocks, 1, chunk, HD), lambda h: (0, h, 0, 0)),
        ),
        scratch_shapes=[
            pltpu.VMEM((span, HD), jnp.bfloat16),
            pltpu.VMEM((span, 2 * HD), jnp.bfloat16),
            pltpu.VMEM((height, span), jnp.float32),
        ],
        compiler_params=pltpu.CompilerParams(vmem_limit_bytes=LIMIT),
        name="attend",
    )(
        queries.reshape(blocks, kv_local, chunk, depth),
        cache_keys,
        cache_values,
        store_cos,
        store_sin,
        news,
        all_pos,
        listed[:, None],
    )

    heads_out = pl.pallas_call(
        functools.partial(combine_kernel, count),
        out_shape=jax.ShapeDtypeStruct((count, chunk, depth), jnp.bfloat16),
        in_specs=[VMEM] * 2,
        out_specs=VMEM,
        scratch_shapes=reduce_scratch(count, chunk, depth, jnp.bfloat16)
        + reduce_scratch(count, chunk, HD, jnp.float32)
        + gather_sems(count),
        compiler_params=pltpu.CompilerParams(
            collective_id=1, has_side_effects=True, vmem_limit_bytes=LIMIT
        ),
        name="combine",
    )(numer.reshape(count, chunk, depth), stats.reshape(count, chunk, HD))

    share = row_count // count
    held = round_up(2 * share, 8)
    given = round_up(share, 16)
    next_wide = next_weight.shape[1]
    hidden_out, next_out = pl.pallas_call(
        functools.partial(output_kernel, count, splits, share),
        out_shape=(
            jax.ShapeDtypeStruct((height, model_part), jnp.bfloat16),
            jax.ShapeDtypeStruct((given, next_wide), jnp.bfloat16),
        ),
        in_specs=[VMEM, VMEM, VMEM, ANY, ANY],
        out_specs=(VMEM, VMEM),
        scratch_shapes=[
            pltpu.VMEM(out_weight.shape, jnp.bfloat16),
            pltpu.VMEM(next_weight.shape, jnp.bfloat16),
            pltpu.SemaphoreType.DMA((2,)),
            pltpu.VMEM((splits, height, model_part), jnp.bfloat16),
            pltpu.SemaphoreType.DMA((splits,)),
            pltpu.SemaphoreType.DMA((splits,)),
            pltpu.VMEM((count, 8, height), jnp.float32),
            pltpu.SemaphoreType.DMA((count,)),
            pltpu.SemaphoreType.DMA((count,)),
            pltpu.VMEM((height, model_part), jnp.float32),
            pltpu.VMEM((count // 2, held, model_part), jnp.float32),
            pltpu.VMEM((given, next_wide // 2), jnp.bfloat16),
            pltpu.VMEM((given, next_wide // 2), jnp.bfloat16),
            pltpu.SemaphoreType.DMA((2,)),
            pltpu.VMEM((count // 2, held, next_wide), jnp.float32),
        ]
        + reduce_scratch(count, held, next_wide // 2, jnp.float32),
        compiler_params=pltpu.CompilerParams(
            collective_id=2, has_side_effects=True, vmem_limit_bytes=LIMIT
        ),
        name="output",
    )(heads_out, hidden, norm_gain[None, :], out_weight, next_weight)
    if chunk != own:
        hidden_out = hidden_out.reshape(blocks, chunk, model_part)[:, :own]
        hidden_out = hidden_out.reshape(row_count, model_part)
    return (hidden_out, next_out[:share])


def solution(mesh):
    in_specs = (
        P(None, "groups"),
        P("groups", "heads"),
        P("heads", "groups"),
        P("groups"),
        P("groups", "heads"),
        P("groups", "heads"),
        P("groups", "heads"),
        P(),
        P(),
        P(),
        P(),
    )
    out_specs = (P(None, "groups"), P("groups", "heads"))
    return jax.shard_map(
        functools.partial(on_device, mesh.shape["groups"], mesh.shape["heads"]),
        mesh=mesh,
        in_specs=in_specs,
        out_specs=out_specs,
        check_vma=False,
    )
```
